32 devices in a mesh: groups: 2 (over y), gx: 16 (over z, x, core).
Axes of the slice: x: 2, y: 2, z: 4, core: 2. Of those that a mesh axis runs over, the one named last changes fastest.
Arguments:
- embeddings: bfloat16 [24576, 1024], P(('groups', 'gx')), parts along dimension 0, may hold values from -16 to 16
- membership: int32 [24576], P(('groups', 'gx')), parts along dimension 0, may hold values 0 or 1
Outputs:
- moved: bfloat16 [24576, 1024], P(('groups', 'gx')), parts along dimension 0
- relative: float32 [24576], P(('groups', 'gx')), parts along dimension 0
The draws below stay inside these ranges and needn't reach their ends.
There are 2 independent parts, one for each index of `groups`. The reference program is written for one: setup_inputs(seed, part) draws one part's arguments, and reference() takes and returns one part's arrays. A program takes and returns all parts, laid end to end along the dimension named above; each array names one. Nothing has to cross between parts.
All inputs are finite; a program needn't handle non-finite values. No bound on the sum of `membership` on one device may be relied on, other than what follows from the above.
Results may differ from the reference program's by a relative error of at most 0.001.
Values may be sent and summed in bfloat16 or wider, within the bound.
A program may use at most 64 MiB of HBM per device.

```python
import jax
import jax.numpy as jnp
from jax import lax

D = 1024
ROWS = 768
BLOCKS = 16
TOTAL = 12288
FIRST = 4
SECOND = 6


def draw_embeddings(key, part):
    key = jax.random.fold_in(key, 11)
    keys = jax.random.split(key, 4)
    labels = jax.random.randint(keys[0], (TOTAL,), 0, 64)
    centers = jnp.clip(jax.random.normal(keys[1], (64, D), jnp.float32), -4.0, 4.0)
    position = jnp.arange(TOTAL, dtype=jnp.float32) / TOTAL
    spread = 0.4 + 0.8 * position
    noise = jnp.clip(jax.random.normal(keys[2], (TOTAL, D), jnp.float32), -4.0, 4.0)
    scales = jnp.exp(jax.random.uniform(keys[3], (TOTAL, 1), jnp.float32, -0.35, 0.35))
    values = scales * (0.7 * centers[labels] + spread[:, None] * noise)
    values = jnp.clip(values, -16.0, 16.0)
    return values.astype(jnp.bfloat16)


def plant(drawn, rng, low, largest):
    spot = [jax.random.randint(jax.random.fold_in(rng, axis), (), 0, length) for axis, length in enumerate(drawn.shape)]
    main_axis = drawn.shape.index(max(drawn.shape))
    next_to = spot[:main_axis] + [(spot[main_axis] + 1) % drawn.shape[main_axis]] + spot[main_axis + 1:]
    return drawn.at[tuple(spot)].set(low).at[tuple(next_to)].set(largest)


def setup_inputs(seed: int = 0, part: int = 0) -> dict:
    key_of = jax.random.split(jax.random.key(seed), 3)
    own_keys = jax.random.split(jax.random.fold_in(key_of[2], part), 3)
    return {
        "embeddings": draw_embeddings(jax.random.fold_in(jax.random.fold_in(key_of[2], part), 71), part),
        "membership": plant((jax.random.randint(own_keys[1], (TOTAL,), 0, 4) < 3).astype(jnp.int32), jax.random.fold_in(own_keys[1], 1), 0, 1),
    }


def pair_terms(rows, row_norms, keys, key_norms, key_member):
    dots = jnp.dot(rows, keys.T, preferred_element_type=jnp.float32)
    dist = row_norms[:, None] + key_norms[None, :] - 2.0 * dots
    weight = jnp.exp(-(4.0 / D) * dist) * key_member[None, :]
    sums = jnp.dot(weight.astype(jnp.bfloat16), keys, preferred_element_type=jnp.float32)
    return jnp.sum(weight, axis=1), sums


def reference(embeddings, membership):
    blocks = embeddings.reshape(BLOCKS, ROWS, D)
    member = membership.astype(jnp.float32).reshape(BLOCKS, ROWS)
    norms = jnp.sum(jnp.square(embeddings.astype(jnp.float32)), axis=1).reshape(BLOCKS, ROWS)

    def one_block(index):
        rows = lax.dynamic_index_in_dim(blocks, index, 0, keepdims=False)
        row_norms = lax.dynamic_index_in_dim(norms, index, 0, keepdims=False)
        density = jnp.zeros((ROWS,), jnp.float32)
        sums = jnp.zeros((ROWS, D), jnp.float32)
        for offset in (0, FIRST, -FIRST, SECOND, -SECOND):
            other = ((index + offset + BLOCKS) % BLOCKS).astype(jnp.int32)
            keys = lax.dynamic_index_in_dim(blocks, other, 0, keepdims=False)
            key_norms = lax.dynamic_index_in_dim(norms, other, 0, keepdims=False)
            key_member = lax.dynamic_index_in_dim(member, other, 0, keepdims=False)
            part_density, part_sums = pair_terms(rows, row_norms, keys, key_norms, key_member)
            density = density + part_density
            sums = sums + part_sums
        return density, sums

    density, sums = lax.map(one_block, jnp.arange(BLOCKS, dtype=jnp.int32))
    density = density.reshape(TOTAL)
    sums = sums.reshape(TOTAL, D)
    moved = (sums / jnp.maximum(density, 1.0)[:, None]).astype(jnp.bfloat16)
    flat_member = member.reshape(TOTAL)
    member_density = jnp.sum(density * flat_member)
    member_count = jnp.sum(flat_member)
    relative = density / (1.0 + member_density / jnp.maximum(member_count, 1.0))
    return moved, relative
```

```python
import functools

import jax
import jax.numpy as jnp
from jax import lax
from jax.experimental import pallas as pl
from jax.experimental.pallas import tpu as pltpu
from jax.sharding import PartitionSpec as P

MESH = pl.DeviceIdType.MESH
CHUNK = 64
LAG = 2
TILE = 384
LANES = 128


def plan(chunks, lag):
    half = chunks // 2
    low, high = list(range(half)), list(range(half, chunks))
    ahead, behind = low + high, high + low
    ready = {}
    done_x, done_pass_a, done_pass_b = set(), set(), set()
    slots = []
    t = 0
    while ahead or behind or len(done_x) < chunks + half or len(done_pass_a) < half or len(done_pass_b) < half:
        now = {key for key, when in ready.items() if when <= t}
        sends = {}
        passed = [k for k in high if (5, k) in now and k not in done_pass_b]
        if passed:
            done_pass_b.add(passed[0])
            sends["ahead"] = ("pass", passed[0])
        elif ahead:
            sends["ahead"] = ("own", ahead.pop(0))
        passed = [k for k in low if (3, k) in now and k not in done_pass_a]
        if passed:
            done_pass_a.add(passed[0])
            sends["behind"] = ("pass", passed[0])
        elif behind:
            sends["behind"] = ("own", behind.pop(0))
        order = [role_chunk for pair in zip([(1, k) for k in low], [(2, k) for k in high]) for role_chunk in pair]
        order += [(1, k) for k in high]
        across = [rc for rc in order if rc in now and rc not in done_x]
        if across:
            done_x.add(across[0])
            sends["across"] = across[0]
        for link, what in sends.items():
            if link == "across":
                key = (3, what[1]) if what[0] == 1 else (5, what[1])
            elif what[0] == "own":
                key = (1, what[1]) if link == "ahead" else (2, what[1])
            else:
                key = (4, what[1])
            ready[key] = t + lag
        slots.append(sends)
        t += 1
    return slots, ready


def kernel(count, e_ref, member_ref, moved_ref, density_ref, held, passing, bias, bias_col, sums, dens,
           recv, send_own, send_x, send_pass, bias_send, bias_recv):
    rows, width = e_ref.shape
    chunks = rows // CHUNK
    half = chunks // 2
    tile = TILE if rows % TILE == 0 else rows
    scale = 4.0 / width
    unit = count // 8
    me = lax.axis_index("gx")
    z = lax.div(me, 2 * unit)
    x = lax.rem(lax.div(me, unit), 2)
    rest = lax.rem(me, unit)
    step = 1 - 2 * x

    def device(up, side):
        return (lax.rem(z + up + 4, 4) * 2 + side) * unit + rest

    ahead = device(step, x)
    behind = device(-step, x)
    across = device(0, 1 - x)
    diagonal = device(step, 1 - x)
    opposite = device(2, 1 - x)

    barrier = pltpu.get_barrier_semaphore()
    for other in (ahead, behind, across, diagonal, opposite):
        pl.semaphore_signal(barrier, inc=1, device_id={"gx": other}, device_id_type=MESH)
    pl.semaphore_wait(barrier, 5)

    def piece(role, k):
        if role == 0:
            return e_ref.at[pl.ds(k * CHUNK, CHUNK)]
        if role == 5:
            return passing.at[pl.ds((k - half) * CHUNK, CHUNK)]
        return held.at[role - 1, pl.ds(k * CHUNK, CHUNK)]

    def copy(source, target, k, sem, other):
        return pltpu.make_async_remote_copy(
            src_ref=piece(source, k), dst_ref=piece(target, k), send_sem=sem, recv_sem=recv.at[target - 1, k],
            device_id={"gx": other}, device_id_type=MESH)

    slots, ready = plan(chunks, LAG)
    copies = []
    arrived = {}

    def wait_for(role, k):
        if (role, k) not in arrived:
            arrived[(role, k)] = True
            copy(role, role, k, send_own.at[0, 0], across).wait_recv()

    def issue(sends):
        for link in ("across", "ahead", "behind"):
            if link not in sends:
                continue
            kind, k = sends[link]
            if link == "across":
                wait_for(kind, k)
                made = copy(kind, 3 if kind == 1 else 5, k, send_x.at[kind - 1, k], across)
            elif kind == "own":
                lane = 0 if link == "ahead" else 1
                made = copy(0, 1 + lane, k, send_own.at[lane, k], ahead if lane == 0 else behind)
            else:
                source = 5 if link == "ahead" else 3
                wait_for(source, k)
                made = copy(source, 4, k, send_pass.at[k], ahead if link == "ahead" else behind)
            made.start()
            copies.append(made)

    def prepare():
        @pl.loop(0, rows // LANES)
        def _(i):
            at = pl.ds(pl.multiple_of(i * LANES, LANES), LANES)
            values = e_ref[at, :].astype(jnp.float32)
            norms = jnp.sum(values * values, axis=1, keepdims=True) * scale
            wide = jnp.broadcast_to(norms, (LANES, LANES))
            bias_col[at, :] = wide
            line = jnp.transpose(wide)[0:1, :]
            bias[0, :, at] = jnp.where(member_ref[:, at] > 0, line, 1e30)
            dens[at, :] = jnp.zeros((LANES, LANES), jnp.float32)

    def compute(role, start, size, first=False):
        @pl.loop(0, rows // 256)
        def _(i):
            at = pl.ds(pl.multiple_of(i * 256, 256), 256)
            keys = e_ref[start:start + size, :] if role == 0 else held[role - 1, start:start + size, :]
            dots = lax.dot_general(e_ref[at, :], keys, (((1,), (1,)), ((), ())), preferred_element_type=jnp.float32)
            own = bias_col[at, :]
            total = dens[at, :]
            parts = []
            for j in range(0, size, LANES):
                dist = own + bias[role, :, start + j:start + j + LANES]
                weight = jnp.exp(2.0 * scale * dots[:, j:j + LANES] - dist)
                total = total + weight
                parts.append(weight.astype(jnp.bfloat16))
            dens[at, :] = total
            low = jnp.concatenate(parts, axis=1) if len(parts) > 1 else parts[0]
            term = jnp.dot(low, keys, preferred_element_type=jnp.float32)
            if first:
                sums[at, :] = term
            else:
                sums[at, :] += term

    def bias_copy(role, other):
        return pltpu.make_async_remote_copy(
            src_ref=bias.at[0], dst_ref=bias.at[role], send_sem=bias_send.at[role - 1], recv_sem=bias_recv.at[role - 1],
            device_id={"gx": other}, device_id_type=MESH)

    bias_ready = set()

    def need_bias(role):
        if role > 0 and role not in bias_ready:
            bias_ready.add(role)
            bias_copy(role, across).wait_recv()

    tiles = []
    for role in range(1, 5):
        for start in range(0, rows, tile):
            ks = range(start // CHUNK, (start + tile) // CHUNK)
            tiles.append((max(ready[(role, k)] for k in ks), role, start))
    tiles.sort()
    own_tiles = list(range(0, rows, tile))

    for t in range(LAG):
        issue(slots[t])
    prepare()
    for role, other in ((1, ahead), (2, behind), (3, diagonal), (4, opposite)):
        made = bias_copy(role, other)
        made.start()
        copies.append(made)

    last = max(ready.values())
    for t in range(LAG, last + 1):
        for key, when in ready.items():
            if when == t:
                wait_for(*key)
        if t < len(slots):
            issue(slots[t])
        if own_tiles:
            start = own_tiles.pop(0)
            compute(0, start, tile, first=start == 0)
        elif tiles and tiles[0][0] <= t:
            _, role, start = tiles.pop(0)
            need_bias(role)
            compute(role, start, tile)
    for _, role, start in tiles:
        need_bias(role)
        compute(role, start, tile)

    @pl.loop(0, rows // LANES)
    def _(i):
        at = pl.ds(pl.multiple_of(i * LANES, LANES), LANES)
        density = jnp.sum(dens[at, :], axis=1, keepdims=True)
        wide = jnp.broadcast_to(density, (LANES, LANES))
        density_ref[:, at] = jnp.transpose(wide)[0:1, :]
        moved_ref[at, :] = (sums[at, :] / jnp.maximum(density, 1.0)).astype(moved_ref.dtype)

    for made in copies:
        made.wait_send()


def shards(count, embeddings, membership):
    rows, width = embeddings.shape
    chunks = rows // CHUNK
    vmem = pl.BlockSpec(memory_space=pltpu.VMEM)
    moved, density = pl.pallas_call(
        functools.partial(kernel, count),
        out_shape=(jax.ShapeDtypeStruct((rows, width), jnp.bfloat16), jax.ShapeDtypeStruct((1, rows), jnp.float32)),
        in_specs=[vmem, vmem],
        out_specs=(vmem, vmem),
        scratch_shapes=[
            pltpu.VMEM((4, rows, width), jnp.bfloat16),
            pltpu.VMEM((rows // 2, width), jnp.bfloat16),
            pltpu.VMEM((5, 1, rows), jnp.float32),
            pltpu.VMEM((rows, LANES), jnp.float32),
            pltpu.VMEM((rows, width), jnp.float32),
            pltpu.VMEM((rows, LANES), jnp.float32),
            pltpu.SemaphoreType.DMA((5, chunks)),
            pltpu.SemaphoreType.DMA((2, chunks)),
            pltpu.SemaphoreType.DMA((2, chunks)),
            pltpu.SemaphoreType.DMA((chunks,)),
            pltpu.SemaphoreType.DMA((4,)),
            pltpu.SemaphoreType.DMA((4,)),
        ],
        compiler_params=pltpu.CompilerParams(collective_id=0, has_side_effects=True, vmem_limit_bytes=48 * 1024 * 1024),
    )(embeddings, membership[None, :])
    density = density[0]
    member = membership.astype(jnp.float32)
    member_density, member_count = lax.psum((jnp.sum(density * member), jnp.sum(member)), "gx")
    relative = density / (1.0 + member_density / jnp.maximum(member_count, 1.0))
    return (moved, relative)


def solution(mesh):
    in_specs = (P(("groups", "gx"), None), P(("groups", "gx")))
    out_specs = (P(("groups", "gx"), None), P(("groups", "gx")))
    step = functools.partial(shards, mesh.shape["gx"])
    return jax.shard_map(step, mesh=mesh, in_specs=in_specs, out_specs=out_specs, check_vma=False)
```

```python
import functools

import jax
import jax.numpy as jnp
from jax import lax
from jax.experimental import pallas as pl
from jax.experimental.pallas import tpu as pltpu
from jax.sharding import PartitionSpec as P

MESH = pl.DeviceIdType.MESH
CHUNK = 64
LAG = 2
TILE = 384
LANES = 128


def plan(chunks, lag):
    half = chunks // 2
    low, high = list(range(half)), list(range(half, chunks))
    ahead, behind = low + high, high + low
    ready = {}
    done_x, done_pass_a, done_pass_b = set(), set(), set()
    slots = []
    t = 0
    while ahead or behind or len(done_x) < chunks + half or len(done_pass_a) < half or len(done_pass_b) < half:
        now = {key for key, when in ready.items() if when <= t}
        sends = {}
        passed = [k for k in high if (5, k) in now and k not in done_pass_b]
        if passed:
            done_pass_b.add(passed[0])
            sends["ahead"] = ("pass", passed[0])
        elif ahead:
            sends["ahead"] = ("own", ahead.pop(0))
        passed = [k for k in low if (3, k) in now and k not in done_pass_a]
        if passed:
            done_pass_a.add(passed[0])
            sends["behind"] = ("pass", passed[0])
        elif behind:
            sends["behind"] = ("own", behind.pop(0))
        order = [role_chunk for pair in zip([(1, k) for k in low], [(2, k) for k in high]) for role_chunk in pair]
        order += [(1, k) for k in high]
        across = [rc for rc in order if rc in now and rc not in done_x]
        if across:
            done_x.add(across[0])
            sends["across"] = across[0]
        for link, what in sends.items():
            if link == "across":
                key = (3, what[1]) if what[0] == 1 else (5, what[1])
            elif what[0] == "own":
                key = (1, what[1]) if link == "ahead" else (2, what[1])
            else:
                key = (4, what[1])
            ready[key] = t + lag
        slots.append(sends)
        t += 1
    return slots, ready


def stages(count):
    out, stride = [], 1
    while stride < count:
        radix = 4 if count // stride % 4 == 0 else 2
        out.append((stride, radix))
        stride *= radix
    return out


def kernel(count, e_ref, member_ref, moved_ref, relative_ref, held, passing, bias, bias_col, sums, dens, density_row, totals,
           recv, send_own, send_x, send_pass, bias_send, bias_recv, total_send, total_recv):
    rows, width = e_ref.shape
    chunks = rows // CHUNK
    half = chunks // 2
    tile = TILE if rows % TILE == 0 else rows
    scale = 4.0 / width
    unit = count // 8
    me = lax.axis_index("gx")
    z = lax.div(me, 2 * unit)
    x = lax.rem(lax.div(me, unit), 2)
    rest = lax.rem(me, unit)
    step = 1 - 2 * x

    def device(up, side):
        return (lax.rem(z + up + 4, 4) * 2 + side) * unit + rest

    ahead = device(step, x)
    behind = device(-step, x)
    across = device(0, 1 - x)
    diagonal = device(step, 1 - x)
    opposite = device(2, 1 - x)

    peers = []
    for stride, radix in stages(count):
        digit = lax.rem(lax.div(me, stride), radix)
        peers.append([me + (lax.rem(digit + d, radix) - digit) * stride for d in range(1, radix)])

    barrier = pltpu.get_barrier_semaphore()
    greeted = [ahead, behind, across, diagonal, opposite] + [other for line in peers for other in line]
    for other in greeted:
        pl.semaphore_signal(barrier, inc=1, device_id={"gx": other}, device_id_type=MESH)
    pl.semaphore_wait(barrier, len(greeted))

    def piece(role, k):
        if role == 0:
            return e_ref.at[pl.ds(k * CHUNK, CHUNK)]
        if role == 5:
            return passing.at[pl.ds((k - half) * CHUNK, CHUNK)]
        return held.at[role - 1, pl.ds(k * CHUNK, CHUNK)]

    def copy(source, target, k, sem, other):
        return pltpu.make_async_remote_copy(
            src_ref=piece(source, k), dst_ref=piece(target, k), send_sem=sem, recv_sem=recv.at[target - 1, k],
            device_id={"gx": other}, device_id_type=MESH)

    slots, ready = plan(chunks, LAG)
    copies = []
    arrived = {}

    def wait_for(role, k):
        if (role, k) not in arrived:
            arrived[(role, k)] = True
            copy(role, role, k, send_own.at[0, 0], across).wait_recv()

    def issue(sends):
        for link in ("across", "ahead", "behind"):
            if link not in sends:
                continue
            kind, k = sends[link]
            if link == "across":
                wait_for(kind, k)
                made = copy(kind, 3 if kind == 1 else 5, k, send_x.at[kind - 1, k], across)
            elif kind == "own":
                lane = 0 if link == "ahead" else 1
                made = copy(0, 1 + lane, k, send_own.at[lane, k], ahead if lane == 0 else behind)
            else:
                source = 5 if link == "ahead" else 3
                wait_for(source, k)
                made = copy(source, 4, k, send_pass.at[k], ahead if link == "ahead" else behind)
            made.start()
            copies.append(made)

    def prepare():
        @pl.loop(0, rows // LANES)
        def _(i):
            at = pl.ds(pl.multiple_of(i * LANES, LANES), LANES)
            values = e_ref[at, :].astype(jnp.float32)
            norms = jnp.sum(values * values, axis=1, keepdims=True) * scale
            wide = jnp.broadcast_to(norms, (LANES, LANES))
            bias_col[at, :] = wide
            line = jnp.transpose(wide)[0:1, :]
            bias[0, :, at] = jnp.where(member_ref[:, at] > 0, line, 1e30)
            dens[at, :] = jnp.zeros((LANES, LANES), jnp.float32)

    def compute(role, start, size, first=False):
        @pl.loop(0, rows // 256)
        def _(i):
            at = pl.ds(pl.multiple_of(i * 256, 256), 256)
            keys = e_ref[start:start + size, :] if role == 0 else held[role - 1, start:start + size, :]
            dots = lax.dot_general(e_ref[at, :], keys, (((1,), (1,)), ((), ())), preferred_element_type=jnp.float32)
            own = bias_col[at, :]
            total = dens[at, :]
            parts = []
            for j in range(0, size, LANES):
                dist = own + bias[role, :, start + j:start + j + LANES]
                weight = jnp.exp(2.0 * scale * dots[:, j:j + LANES] - dist)
                total = total + weight
                parts.append(weight.astype(jnp.bfloat16))
            dens[at, :] = total
            low = jnp.concatenate(parts, axis=1) if len(parts) > 1 else parts[0]
            term = jnp.dot(low, keys, preferred_element_type=jnp.float32)
            if first:
                sums[at, :] = term
            else:
                sums[at, :] += term

    def bias_copy(role, other):
        return pltpu.make_async_remote_copy(
            src_ref=bias.at[0], dst_ref=bias.at[role], send_sem=bias_send.at[role - 1], recv_sem=bias_recv.at[role - 1],
            device_id={"gx": other}, device_id_type=MESH)

    bias_ready = set()

    def need_bias(role):
        if role > 0 and role not in bias_ready:
            bias_ready.add(role)
            bias_copy(role, across).wait_recv()

    tiles = []
    for role in range(1, 5):
        for start in range(0, rows, tile):
            ks = range(start // CHUNK, (start + tile) // CHUNK)
            tiles.append((max(ready[(role, k)] for k in ks), role, start))
    tiles.sort()
    own_tiles = list(range(0, rows, tile))

    for t in range(LAG):
        issue(slots[t])
    prepare()
    for role, other in ((1, ahead), (2, behind), (3, diagonal), (4, opposite)):
        made = bias_copy(role, other)
        made.start()
        copies.append(made)

    last = max(ready.values())
    for t in range(LAG, last + 1):
        for key, when in ready.items():
            if when == t:
                wait_for(*key)
        if t < len(slots):
            issue(slots[t])
        if own_tiles:
            start = own_tiles.pop(0)
            compute(0, start, tile, first=start == 0)
        elif tiles and tiles[0][0] <= t:
            _, role, start = tiles.pop(0)
            need_bias(role)
            compute(role, start, tile)
    for _, role, start in tiles:
        need_bias(role)
        compute(role, start, tile)

    @pl.loop(0, rows // LANES)
    def _(i):
        at = pl.ds(pl.multiple_of(i * LANES, LANES), LANES)
        density = jnp.broadcast_to(jnp.sum(dens[at, :], axis=1, keepdims=True), (LANES, LANES))
        dens[at, :] = density
        density_row[:, at] = jnp.transpose(density)[0:1, :]

    def exchange(stage):
        made = []
        for d, other in enumerate(peers[stage], 1):
            made.append(pltpu.make_async_remote_copy(
                src_ref=totals.at[stage, 0], dst_ref=totals.at[stage, d], send_sem=total_send.at[stage, d - 1],
                recv_sem=total_recv.at[stage, d - 1], device_id={"gx": other}, device_id_type=MESH))
            made[-1].start()
        return made

    member = member_ref[...].astype(jnp.float32)
    local_density = jnp.sum(density_row[...] * member, axis=1, keepdims=True)
    local_count = jnp.sum(member, axis=1, keepdims=True)
    first_line = lax.broadcasted_iota(jnp.int32, (8, LANES), 0) == 0
    totals[0, 0] = jnp.where(first_line, jnp.broadcast_to(local_density, (8, LANES)), jnp.broadcast_to(local_count, (8, LANES)))
    flying = exchange(0)

    @pl.loop(0, rows // LANES)
    def _(i):
        at = pl.ds(pl.multiple_of(i * LANES, LANES), LANES)
        moved_ref[at, :] = (sums[at, :] / jnp.maximum(dens[at, 0:1], 1.0)).astype(moved_ref.dtype)

    for stage in range(len(peers)):
        for made in flying:
            made.wait()
        total = totals[stage, 0]
        for d in range(1, len(peers[stage]) + 1):
            total = total + totals[stage, d]
        if stage + 1 < len(peers):
            totals[stage + 1, 0] = total
            flying = exchange(stage + 1)
    mean = total[0:1, 0:1] / jnp.maximum(total[1:2, 0:1], 1.0)
    relative_ref[...] = density_row[...] / (1.0 + mean)

    for made in copies:
        made.wait_send()


def shards(count, embeddings, membership):
    rows, width = embeddings.shape
    chunks = rows // CHUNK
    vmem = pl.BlockSpec(memory_space=pltpu.VMEM)
    count_stages = len(stages(count))
    moved, relative = pl.pallas_call(
        functools.partial(kernel, count),
        out_shape=(jax.ShapeDtypeStruct((rows, width), jnp.bfloat16), jax.ShapeDtypeStruct((1, rows), jnp.float32)),
        in_specs=[vmem, vmem],
        out_specs=(vmem, vmem),
        scratch_shapes=[
            pltpu.VMEM((4, rows, width), jnp.bfloat16),
            pltpu.VMEM((rows // 2, width), jnp.bfloat16),
            pltpu.VMEM((5, 1, rows), jnp.float32),
            pltpu.VMEM((rows, LANES), jnp.float32),
            pltpu.VMEM((rows, width), jnp.float32),
            pltpu.VMEM((rows, LANES), jnp.float32),
            pltpu.VMEM((1, rows), jnp.float32),
            pltpu.VMEM((count_stages, 4, 8, LANES), jnp.float32),
            pltpu.SemaphoreType.DMA((5, chunks)),
            pltpu.SemaphoreType.DMA((2, chunks)),
            pltpu.SemaphoreType.DMA((2, chunks)),
            pltpu.SemaphoreType.DMA((chunks,)),
            pltpu.SemaphoreType.DMA((4,)),
            pltpu.SemaphoreType.DMA((4,)),
            pltpu.SemaphoreType.DMA((count_stages, 3)),
            pltpu.SemaphoreType.DMA((count_stages, 3)),
        ],
        compiler_params=pltpu.CompilerParams(collective_id=0, has_side_effects=True, vmem_limit_bytes=48 * 1024 * 1024),
    )(embeddings, membership[None, :])
    return (moved, relative[0])


def solution(mesh):
    in_specs = (P(("groups", "gx"), None), P(("groups", "gx")))
    out_specs = (P(("groups", "gx"), None), P(("groups", "gx")))
    step = functools.partial(shards, mesh.shape["gx"])
    return jax.shard_map(step, mesh=mesh, in_specs=in_specs, out_specs=out_specs, check_vma=False)
```

```python
import functools

import jax
import jax.numpy as jnp
from jax import lax
from jax.experimental import pallas as pl
from jax.experimental.pallas import tpu as pltpu
from jax.sharding import PartitionSpec as P

MESH = pl.DeviceIdType.MESH
CHUNK = 64
LAG = 2
TILE = 384
LANES = 128


def slot_of(stream, distance):
    return stream if distance == 1 else distance


def stages(count):
    out, stride = [], 1
    while stride < count:
        radix = 4 if count // stride % 4 == 0 else 2
        out.append((stride, radix))
        stride *= radix
    return out


def kernel(count, e_ref, member_ref, moved_ref, relative_ref, held, bias, bias_col, sums, dens, density_row, totals,
           recv, send_stream, send_x, bias_send, bias_recv, total_send, total_recv):
    rows, width = e_ref.shape
    chunks = rows // CHUNK
    tile = TILE if rows % TILE == 0 else rows
    scale = 4.0 / width
    unit = count // 8
    me = lax.axis_index("gx")
    z = lax.div(me, 2 * unit)
    x = lax.rem(lax.div(me, unit), 2)
    rest = lax.rem(me, unit)
    step = 1 - 2 * x

    def device(up, side):
        return (lax.rem(z + up + 4, 4) * 2 + side) * unit + rest

    above = device(1, x)
    below = device(-1, x)
    across = device(0, 1 - x)
    diagonal = device(step, 1 - x)
    opposite = device(2, 1 - x)

    peers = []
    for stride, radix in stages(count):
        digit = lax.rem(lax.div(me, stride), radix)
        peers.append([me + (lax.rem(digit + d, radix) - digit) * stride for d in range(1, radix)])

    barrier = pltpu.get_barrier_semaphore()
    greeted = [above, below, across, diagonal, opposite] + [other for line in peers for other in line]
    for other in greeted:
        pl.semaphore_signal(barrier, inc=1, device_id={"gx": other}, device_id_type=MESH)
    pl.semaphore_wait(barrier, len(greeted))

    def piece(slot, k):
        if slot is None:
            return e_ref.at[pl.ds(k * CHUNK, CHUNK)]
        return held.at[slot, pl.ds(k * CHUNK, CHUNK)]

    def copy(source, target, k, sem, other):
        return pltpu.make_async_remote_copy(
            src_ref=piece(source, k), dst_ref=piece(target, k), send_sem=sem, recv_sem=recv.at[target, k],
            device_id={"gx": other}, device_id_type=MESH)

    def exists(stream, distance):
        return z >= distance if stream == 0 else z <= 3 - distance

    def sends(stream, distance):
        return z < 4 - 1 if (stream, distance) == (0, 0) else z > 0 if (stream, distance) == (1, 0) else (
            jnp.logical_and(exists(stream, distance), z < 3 if stream == 0 else z > 0))

    def crosses(stream, distance):
        there = exists(stream, distance)
        if distance == 2:
            return there
        return jnp.logical_and(there, x == (stream if distance == 1 else 1 - stream))

    def crossing(stream, distance):
        there = exists(stream, distance)
        if distance == 2:
            return there
        return jnp.logical_and(there, x == (1 - stream if distance == 1 else stream))

    def stream_copy(stream, position):
        distance, k = position // chunks, position % chunks
        source = None if distance == 0 else slot_of(stream, distance)
        return copy(source, slot_of(stream, distance + 1), k, send_stream.at[stream, distance, k], above if stream == 0 else below)

    def cross_copy(stream, distance, k):
        side = 1 if distance == 2 else 0
        return copy(slot_of(stream, distance), 4 + side, k, send_x.at[side, k], across)

    def wait_slot(slot, k):
        copy(slot, slot, k, send_x.at[0, 0], across).wait_recv()

    def step_streams(t):
        for stream in (0, 1):
            position = t - LAG
            if 0 <= position < 3 * chunks:
                distance, k = position // chunks + 1, position % chunks

                @pl.when(exists(stream, distance))
                def _():
                    wait_slot(slot_of(stream, distance), k)

                @pl.when(crosses(stream, distance))
                def _():
                    cross_copy(stream, distance, k).start()

            if t < 3 * chunks:
                @pl.when(sends(stream, t // chunks))
                def _():
                    stream_copy(stream, t).start()

    def prepare():
        @pl.loop(0, rows // LANES)
        def _(i):
            at = pl.ds(pl.multiple_of(i * LANES, LANES), LANES)
            values = e_ref[at, :].astype(jnp.float32)
            norms = jnp.sum(values * values, axis=1, keepdims=True) * scale
            wide = jnp.broadcast_to(norms, (LANES, LANES))
            bias_col[at, :] = wide
            line = jnp.transpose(wide)[0:1, :]
            bias[0, :, at] = jnp.where(member_ref[:, at] > 0, line, 1e30)
            dens[at, :] = jnp.zeros((LANES, LANES), jnp.float32)

    def compute(slot, role, start, size, first=False):
        @pl.loop(0, rows // 256)
        def _(i):
            at = pl.ds(pl.multiple_of(i * 256, 256), 256)
            keys = e_ref[start:start + size, :] if slot is None else held[slot, start:start + size, :]
            dots = lax.dot_general(e_ref[at, :], keys, (((1,), (1,)), ((), ())), preferred_element_type=jnp.float32)
            own = bias_col[at, :]
            total = dens[at, :]
            parts = []
            for j in range(0, size, LANES):
                dist = own + bias[role, :, start + j:start + j + LANES]
                weight = jnp.exp(2.0 * scale * dots[:, j:j + LANES] - dist)
                total = total + weight
                parts.append(weight.astype(jnp.bfloat16))
            dens[at, :] = total
            low = jnp.concatenate(parts, axis=1) if len(parts) > 1 else parts[0]
            term = jnp.dot(low, keys, preferred_element_type=jnp.float32)
            if first:
                sums[at, :] = term
            else:
                sums[at, :] += term

    def bias_copy(role, other):
        return pltpu.make_async_remote_copy(
            src_ref=bias.at[0], dst_ref=bias.at[role], send_sem=bias_send.at[role - 1], recv_sem=bias_recv.at[role - 1],
            device_id={"gx": other}, device_id_type=MESH)

    def split(distance):
        if distance == 3 and rows == 768:
            return [(0, 384), (384, 256), (640, 128)]
        return [(start, tile) for start in range(0, rows, tile)]

    wrapped = jnp.where(z == 0, 1, 2)
    tiles = []
    for distance in (1, 2, 3):
        for start, size in split(distance):
            when = (distance - 1) * chunks + (start + size) // CHUNK - 1 + LAG
            either = jnp.logical_or(crossing(0, distance), crossing(1, distance))
            if distance == 1:
                tiles.append((when, exists(0, 1), 0, 1, start, size, False))
                tiles.append((when, exists(1, 1), 1, 2, start, size, False))
                tiles.append((when + LAG, either, 4, 3, start, size, True))
            elif distance == 2:
                tiles.append((when + LAG, None, 5, 4, start, size, True))
            else:
                tiles.append((when, jnp.logical_or(z == 0, z == 3), 3, wrapped, start, size, False))
                tiles.append((when + LAG, either, 4, 3, start, size, True))
    tiles.sort(key=lambda item: item[0])

    def run(item):
        _, condition, slot, role, start, size, crossed = item

        def body():
            if crossed:
                for k in range(start // CHUNK, (start + size) // CHUNK):
                    wait_slot(slot, k)
            compute(slot, role, start, size)

        if condition is None:
            body()
        else:
            pl.when(condition)(body)

    own_tiles = list(range(0, rows, tile))
    for t in range(LAG):
        step_streams(t)
    prepare()
    bias_copies = [bias_copy(role, other) for role, other in ((1, above), (2, below), (3, diagonal), (4, opposite))]
    for made in bias_copies:
        made.start()
    for t in range(LAG, 3 * chunks + LAG):
        step_streams(t)
        if own_tiles:
            start = own_tiles.pop(0)
            compute(None, 0, start, tile, first=start == 0)
            if not own_tiles:
                for made in bias_copies:
                    made.wait_recv()
            continue
        done = 0
        while tiles and tiles[0][0] <= t and done < 2:
            run(tiles.pop(0))
            done += 1
    for item in tiles:
        run(item)

    @pl.loop(0, rows // LANES)
    def _(i):
        at = pl.ds(pl.multiple_of(i * LANES, LANES), LANES)
        density = jnp.broadcast_to(jnp.sum(dens[at, :], axis=1, keepdims=True), (LANES, LANES))
        dens[at, :] = density
        density_row[:, at] = jnp.transpose(density)[0:1, :]

    def exchange(stage):
        made = []
        for d, other in enumerate(peers[stage], 1):
            made.append(pltpu.make_async_remote_copy(
                src_ref=totals.at[stage, 0], dst_ref=totals.at[stage, d], send_sem=total_send.at[stage, d - 1],
                recv_sem=total_recv.at[stage, d - 1], device_id={"gx": other}, device_id_type=MESH))
            made[-1].start()
        return made

    member = member_ref[...].astype(jnp.float32)
    local_density = jnp.sum(density_row[...] * member, axis=1, keepdims=True)
    local_count = jnp.sum(member, axis=1, keepdims=True)
    first_line = lax.broadcasted_iota(jnp.int32, (8, LANES), 0) == 0
    totals[0, 0] = jnp.where(first_line, jnp.broadcast_to(local_density, (8, LANES)), jnp.broadcast_to(local_count, (8, LANES)))
    flying = exchange(0)

    @pl.loop(0, rows // LANES)
    def _(i):
        at = pl.ds(pl.multiple_of(i * LANES, LANES), LANES)
        moved_ref[at, :] = (sums[at, :] / jnp.maximum(dens[at, 0:1], 1.0)).astype(moved_ref.dtype)

    for stage in range(len(peers)):
        for made in flying:
            made.wait()
        total = totals[stage, 0]
        for d in range(1, len(peers[stage]) + 1):
            total = total + totals[stage, d]
        if stage + 1 < len(peers):
            totals[stage + 1, 0] = total
            flying = exchange(stage + 1)
    mean = total[0:1, 0:1] / jnp.maximum(total[1:2, 0:1], 1.0)
    relative_ref[...] = density_row[...] / (1.0 + mean)

    for made in bias_copies:
        made.wait_send()
    for stream in (0, 1):
        for distance in range(3):
            @pl.when(sends(stream, distance))
            def _():
                for k in range(chunks):
                    stream_copy(stream, distance * chunks + k).wait_send()

            @pl.when(crosses(stream, distance + 1))
            def _():
                for k in range(chunks):
                    cross_copy(stream, distance + 1, k).wait_send()


def shards(count, embeddings, membership):
    rows, width = embeddings.shape
    chunks = rows // CHUNK
    vmem = pl.BlockSpec(memory_space=pltpu.VMEM)
    count_stages = len(stages(count))
    moved, relative = pl.pallas_call(
        functools.partial(kernel, count),
        out_shape=(jax.ShapeDtypeStruct((rows, width), jnp.bfloat16), jax.ShapeDtypeStruct((1, rows), jnp.float32)),
        in_specs=[vmem, vmem],
        out_specs=(vmem, vmem),
        scratch_shapes=[
            pltpu.VMEM((6, rows, width), jnp.bfloat16),
            pltpu.VMEM((5, 1, rows), jnp.float32),
            pltpu.VMEM((rows, LANES), jnp.float32),
            pltpu.VMEM((rows, width), jnp.float32),
            pltpu.VMEM((rows, LANES), jnp.float32),
            pltpu.VMEM((1, rows), jnp.float32),
            pltpu.VMEM((count_stages, 4, 8, LANES), jnp.float32),
            pltpu.SemaphoreType.DMA((6, chunks)),
            pltpu.SemaphoreType.DMA((2, 3, chunks)),
            pltpu.SemaphoreType.DMA((2, chunks)),
            pltpu.SemaphoreType.DMA((4,)),
            pltpu.SemaphoreType.DMA((4,)),
            pltpu.SemaphoreType.DMA((count_stages, 3)),
            pltpu.SemaphoreType.DMA((count_stages, 3)),
        ],
        compiler_params=pltpu.CompilerParams(collective_id=0, has_side_effects=True, vmem_limit_bytes=48 * 1024 * 1024),
    )(embeddings, membership[None, :])
    return (moved, relative[0])


def solution(mesh):
    in_specs = (P(("groups", "gx"), None), P(("groups", "gx")))
    out_specs = (P(("groups", "gx"), None), P(("groups", "gx")))
    step = functools.partial(shards, mesh.shape["gx"])
    return jax.shard_map(step, mesh=mesh, in_specs=in_specs, out_specs=out_specs, check_vma=False)
```

```python
import functools

import jax
import jax.numpy as jnp
from jax import lax
from jax.experimental import pallas as pl
from jax.experimental.pallas import tpu as pltpu
from jax.sharding import PartitionSpec as P

MESH = pl.DeviceIdType.MESH
CHUNK = 64
LAG = 6
TILE = 384
LANES = 128


def slot_of(stream, distance):
    return stream if distance == 1 else distance


def stages(count):
    out, stride = [], 1
    while stride < count:
        radix = 4 if count // stride % 4 == 0 else 2
        out.append((stride, radix))
        stride *= radix
    return out


def kernel(count, e_ref, member_ref, moved_ref, relative_ref, held, bias, bias_col, sums, dens, density_row, totals,
           recv, send_stream, send_x, bias_send, bias_recv, total_send, total_recv):
    rows, width = e_ref.shape
    chunks = rows // CHUNK
    tile = TILE if rows % TILE == 0 else rows
    scale = 4.0 / width
    unit = count // 8
    me = lax.axis_index("gx")
    z = lax.div(me, 2 * unit)
    x = lax.rem(lax.div(me, unit), 2)
    rest = lax.rem(me, unit)
    step = 1 - 2 * x

    def device(up, side):
        return (lax.rem(z + up + 4, 4) * 2 + side) * unit + rest

    above = device(1, x)
    below = device(-1, x)
    across = device(0, 1 - x)
    diagonal = device(step, 1 - x)
    opposite = device(2, 1 - x)

    peers = []
    for stride, radix in stages(count):
        digit = lax.rem(lax.div(me, stride), radix)
        peers.append([me + (lax.rem(digit + d, radix) - digit) * stride for d in range(1, radix)])

    barrier = pltpu.get_barrier_semaphore()
    greeted = [above, below, across, diagonal, opposite] + [other for line in peers for other in line]
    for other in greeted:
        pl.semaphore_signal(barrier, inc=1, device_id={"gx": other}, device_id_type=MESH)
    pl.semaphore_wait(barrier, len(greeted))

    def piece(slot, k):
        if slot is None:
            return e_ref.at[pl.ds(k * CHUNK, CHUNK)]
        return held.at[slot, pl.ds(k * CHUNK, CHUNK)]

    def copy(source, target, k, sem, other):
        return pltpu.make_async_remote_copy(
            src_ref=piece(source, k), dst_ref=piece(target, k), send_sem=sem, recv_sem=recv.at[target, k],
            device_id={"gx": other}, device_id_type=MESH)

    def exists(stream, distance):
        return z >= distance if stream == 0 else z <= 3 - distance

    def sends(stream, distance):
        return z < 4 - 1 if (stream, distance) == (0, 0) else z > 0 if (stream, distance) == (1, 0) else (
            jnp.logical_and(exists(stream, distance), z < 3 if stream == 0 else z > 0))

    def crosses(stream, distance):
        there = exists(stream, distance)
        if distance == 2:
            return there
        return jnp.logical_and(there, x == (stream if distance == 1 else 1 - stream))

    def crossing(stream, distance):
        there = exists(stream, distance)
        if distance == 2:
            return there
        return jnp.logical_and(there, x == (1 - stream if distance == 1 else stream))

    def stream_copy(stream, position):
        distance, k = position // chunks, position % chunks
        source = None if distance == 0 else slot_of(stream, distance)
        return copy(source, slot_of(stream, distance + 1), k, send_stream.at[stream, distance, k], above if stream == 0 else below)

    def cross_copy(stream, distance, k):
        side = 1 if distance == 2 else 0
        return copy(slot_of(stream, distance), 4 + side, k, send_x.at[side, k], across)

    def wait_slot(slot, k):
        copy(slot, slot, k, send_x.at[0, 0], across).wait_recv()

    def step_streams(t):
        for stream in (0, 1):
            position = t - LAG
            if 0 <= position < 3 * chunks:
                distance, k = position // chunks + 1, position % chunks

                @pl.when(exists(stream, distance))
                def _():
                    wait_slot(slot_of(stream, distance), k)

                @pl.when(crosses(stream, distance))
                def _():
                    cross_copy(stream, distance, k).start()

            if t < 3 * chunks:
                @pl.when(sends(stream, t // chunks))
                def _():
                    stream_copy(stream, t).start()

    def prepare():
        @pl.loop(0, rows // LANES)
        def _(i):
            at = pl.ds(pl.multiple_of(i * LANES, LANES), LANES)
            values = e_ref[at, :].astype(jnp.float32)
            norms = jnp.sum(values * values, axis=1, keepdims=True) * scale
            wide = jnp.broadcast_to(norms, (LANES, LANES))
            bias_col[at, :] = wide
            line = jnp.transpose(wide)[0:1, :]
            bias[0, :, at] = jnp.where(member_ref[:, at] > 0, line, 1e30)
            dens[at, :] = jnp.zeros((LANES, LANES), jnp.float32)

    def compute(slot, role, start, size, first=False):
        @pl.loop(0, rows // 256)
        def _(i):
            at = pl.ds(pl.multiple_of(i * 256, 256), 256)
            keys = e_ref[start:start + size, :] if slot is None else held[slot, start:start + size, :]
            dots = lax.dot_general(e_ref[at, :], keys, (((1,), (1,)), ((), ())), preferred_element_type=jnp.float32)
            own = bias_col[at, :]
            total = dens[at, :]
            parts = []
            for j in range(0, size, LANES):
                dist = own + bias[role, :, start + j:start + j + LANES]
                weight = jnp.exp(2.0 * scale * dots[:, j:j + LANES] - dist)
                total = total + weight
                parts.append(weight.astype(jnp.bfloat16))
            dens[at, :] = total
            low = jnp.concatenate(parts, axis=1) if len(parts) > 1 else parts[0]
            term = jnp.dot(low, keys, preferred_element_type=jnp.float32)
            if first:
                sums[at, :] = term
            else:
                sums[at, :] += term

    def bias_copy(role, other):
        return pltpu.make_async_remote_copy(
            src_ref=bias.at[0], dst_ref=bias.at[role], send_sem=bias_send.at[role - 1], recv_sem=bias_recv.at[role - 1],
            device_id={"gx": other}, device_id_type=MESH)

    def split(distance):
        if distance == 3 and rows == 768:
            return [(0, 384), (384, 256), (640, 128)]
        return [(start, tile) for start in range(0, rows, tile)]

    wrapped = jnp.where(z == 0, 1, 2)
    tiles = []
    for distance in (1, 2, 3):
        for start, size in split(distance):
            when = (distance - 1) * chunks + (start + size) // CHUNK - 1 + LAG
            either = jnp.logical_or(crossing(0, distance), crossing(1, distance))
            if distance == 1:
                tiles.append((when, exists(0, 1), 0, 1, start, size, False))
                tiles.append((when, exists(1, 1), 1, 2, start, size, False))
                tiles.append((when + LAG, either, 4, 3, start, size, True))
            elif distance == 2:
                tiles.append((when + LAG, None, 5, 4, start, size, True))
            else:
                tiles.append((when, jnp.logical_or(z == 0, z == 3), 3, wrapped, start, size, False))
                tiles.append((when + LAG, either, 4, 3, start, size, True))
    tiles.sort(key=lambda item: item[0])

    def run(item):
        _, condition, slot, role, start, size, crossed = item

        def body():
            if crossed:
                for k in range(start // CHUNK, (start + size) // CHUNK):
                    wait_slot(slot, k)
            compute(slot, role, start, size)

        if condition is None:
            body()
        else:
            pl.when(condition)(body)

    own_tiles = list(range(0, rows, tile))
    for t in range(LAG):
        step_streams(t)
    prepare()
    bias_copies = [bias_copy(role, other) for role, other in ((1, above), (2, below), (3, diagonal), (4, opposite))]
    for made in bias_copies:
        made.start()
    for t in range(LAG, 3 * chunks + LAG):
        step_streams(t)
        if own_tiles:
            start = own_tiles.pop(0)
            compute(None, 0, start, tile, first=start == 0)
            if not own_tiles:
                for made in bias_copies:
                    made.wait_recv()
            continue
        done = 0
        while tiles and tiles[0][0] <= t and done < 2:
            run(tiles.pop(0))
            done += 1
    for item in tiles:
        run(item)

    @pl.loop(0, rows // LANES)
    def _(i):
        at = pl.ds(pl.multiple_of(i * LANES, LANES), LANES)
        density = jnp.broadcast_to(jnp.sum(dens[at, :], axis=1, keepdims=True), (LANES, LANES))
        dens[at, :] = density
        density_row[:, at] = jnp.transpose(density)[0:1, :]

    def exchange(stage):
        made = []
        for d, other in enumerate(peers[stage], 1):
            made.append(pltpu.make_async_remote_copy(
                src_ref=totals.at[stage, 0], dst_ref=totals.at[stage, d], send_sem=total_send.at[stage, d - 1],
                recv_sem=total_recv.at[stage, d - 1], device_id={"gx": other}, device_id_type=MESH))
            made[-1].start()
        return made

    member = member_ref[...].astype(jnp.float32)
    local_density = jnp.sum(density_row[...] * member, axis=1, keepdims=True)
    local_count = jnp.sum(member, axis=1, keepdims=True)
    first_line = lax.broadcasted_iota(jnp.int32, (8, LANES), 0) == 0
    totals[0, 0] = jnp.where(first_line, jnp.broadcast_to(local_density, (8, LANES)), jnp.broadcast_to(local_count, (8, LANES)))
    flying = exchange(0)

    @pl.loop(0, rows // LANES)
    def _(i):
        at = pl.ds(pl.multiple_of(i * LANES, LANES), LANES)
        moved_ref[at, :] = (sums[at, :] / jnp.maximum(dens[at, 0:1], 1.0)).astype(moved_ref.dtype)

    for stage in range(len(peers)):
        for made in flying:
            made.wait()
        total = totals[stage, 0]
        for d in range(1, len(peers[stage]) + 1):
            total = total + totals[stage, d]
        if stage + 1 < len(peers):
            totals[stage + 1, 0] = total
            flying = exchange(stage + 1)
    mean = total[0:1, 0:1] / jnp.maximum(total[1:2, 0:1], 1.0)
    relative_ref[...] = density_row[...] / (1.0 + mean)

    for made in bias_copies:
        made.wait_send()
    for stream in (0, 1):
        for distance in range(3):
            @pl.when(sends(stream, distance))
            def _():
                for k in range(chunks):
                    stream_copy(stream, distance * chunks + k).wait_send()

            @pl.when(crosses(stream, distance + 1))
            def _():
                for k in range(chunks):
                    cross_copy(stream, distance + 1, k).wait_send()


def shards(count, embeddings, membership):
    rows, width = embeddings.shape
    chunks = rows // CHUNK
    vmem = pl.BlockSpec(memory_space=pltpu.VMEM)
    count_stages = len(stages(count))
    moved, relative = pl.pallas_call(
        functools.partial(kernel, count),
        out_shape=(jax.ShapeDtypeStruct((rows, width), jnp.bfloat16), jax.ShapeDtypeStruct((1, rows), jnp.float32)),
        in_specs=[vmem, vmem],
        out_specs=(vmem, vmem),
        scratch_shapes=[
            pltpu.VMEM((6, rows, width), jnp.bfloat16),
            pltpu.VMEM((5, 1, rows), jnp.float32),
            pltpu.VMEM((rows, LANES), jnp.float32),
            pltpu.VMEM((rows, width), jnp.float32),
            pltpu.VMEM((rows, LANES), jnp.float32),
            pltpu.VMEM((1, rows), jnp.float32),
            pltpu.VMEM((count_stages, 4, 8, LANES), jnp.float32),
            pltpu.SemaphoreType.DMA((6, chunks)),
            pltpu.SemaphoreType.DMA((2, 3, chunks)),
            pltpu.SemaphoreType.DMA((2, chunks)),
            pltpu.SemaphoreType.DMA((4,)),
            pltpu.SemaphoreType.DMA((4,)),
            pltpu.SemaphoreType.DMA((count_stages, 3)),
            pltpu.SemaphoreType.DMA((count_stages, 3)),
        ],
        compiler_params=pltpu.CompilerParams(collective_id=0, has_side_effects=True, vmem_limit_bytes=48 * 1024 * 1024),
    )(embeddings, membership[None, :])
    return (moved, relative[0])


def solution(mesh):
    in_specs = (P(("groups", "gx"), None), P(("groups", "gx")))
    out_specs = (P(("groups", "gx"), None), P(("groups", "gx")))
    step = functools.partial(shards, mesh.shape["gx"])
    return jax.shard_map(step, mesh=mesh, in_specs=in_specs, out_specs=out_specs, check_vma=False)
```
